32 devices in a mesh: groups: 2 (over y), wide: 4 (over z), narrow: 4 (over x, core).
Axes of the slice: x: 2, y: 2, z: 4, core: 2. Of those that a mesh axis runs over, the one named last changes fastest.
Arguments:
- tokens: bfloat16 [256, 8192], P(('groups', 'wide'), 'narrow'), parts along dimension 0, may hold values from -6 to 6
- gate_weight: bfloat16 [8192, 16384], P('narrow', 'wide'), may hold values from -0.09375 to 0.09375
- up_weight: bfloat16 [8192, 16384], P('narrow', 'wide'), may hold values from -0.09375 to 0.09375
- down_weight: bfloat16 [16384, 8192], P('wide', 'narrow'), may hold values from -0.0625 to 0.0625
- gate_keep: int32 [64, 128], P('narrow', 'wide'), may hold values from 0 to 1, as said below
- up_keep: int32 [64, 128], P('narrow', 'wide'), may hold values from 0 to 1, as said below
- down_keep: int32 [128, 64], P('wide', 'narrow'), may hold values from 0 to 1, as said below
Outputs:
- mixed: bfloat16 [256, 8192], P(('groups', 'wide'), 'narrow'), parts along dimension 0
The draws below stay inside these ranges and needn't reach their ends.
There are 2 independent parts, one for each index of `groups`. The reference program is written for one: setup_inputs(seed, part) draws one part's arguments, and reference() takes and returns one part's arrays. A program takes and returns all parts, laid end to end along the dimension named above; an argument that names none is the same for every part. Nothing has to cross between parts.
Inputs may be any that keep to these rules, and one draw needn't show every extreme that they name: `gate_keep`: 1 keeps a 128 x 128 block of the gate projection, 0 prunes it; the share kept differs between the tiles of blocks that the devices hold. `up_keep`: as for gate_keep, for the up projection. `down_keep`: as for gate_keep, for the down projection.
All inputs are finite; a program needn't handle non-finite values.
Results may differ from the reference program's by a relative error of at most 0.02.
Values may be sent and summed in bfloat16 or wider, within the bound.
A program may use at most 192 MiB of HBM per device.

```python
import jax
import jax.numpy as jnp
from jax import lax

D = 8192
FF = 16384
BLOCK = 128
TOKENS = 128
N_WIDE = 4
N_NARROW = 4


def keep_blocks(key, rows, cols, tile_rows, tile_cols):
    rate_key, roll_key = jax.random.split(key)
    rates = jax.random.randint(rate_key, (rows // tile_rows, cols // tile_cols), 25, 76)
    spread = jnp.repeat(jnp.repeat(rates, tile_rows, axis=0), tile_cols, axis=1)
    rolled = jax.random.randint(roll_key, (rows, cols), 0, 100)
    return (rolled < spread).astype(jnp.int32)


def draw_gate_keep(key, part):
    key = jax.random.fold_in(key, 11)
    return keep_blocks(key, D // BLOCK, FF // BLOCK, D // BLOCK // N_NARROW, FF // BLOCK // N_WIDE)


def draw_up_keep(key, part):
    key = jax.random.fold_in(key, 23)
    return keep_blocks(key, D // BLOCK, FF // BLOCK, D // BLOCK // N_NARROW, FF // BLOCK // N_WIDE)


def draw_down_keep(key, part):
    key = jax.random.fold_in(key, 37)
    return keep_blocks(key, FF // BLOCK, D // BLOCK, FF // BLOCK // N_WIDE, D // BLOCK // N_NARROW)


def shard_levels(key, dims, shards, smallest, high):
    def one(dim, parts):
        draws = jax.random.uniform(jax.random.fold_in(jax.random.fold_in(key, 6), dim), (parts,), jnp.float32, smallest / len(shards), high / len(shards))
        return jnp.repeat(jnp.exp(draws), dims[dim] // parts).reshape((-1,) + (1,) * (len(dims) - dim - 1))

    factor_of = one(*shards[0])
    for cut in shards[1:]:
        factor_of = factor_of * one(*cut)
    return factor_of


def bell_draw(key, shape, scale, bound, shards=(), kind=jnp.bfloat16):
    loudness = shard_levels(key, shape, shards, -0.22, 0.18) if shards else 1.0
    drawn = jax.random.normal(key, shape, jnp.float32) * scale * loudness
    return jnp.minimum(jnp.maximum(drawn, -bound), bound).astype(kind)


def setup_inputs(seed: int = 0, part: int = 0) -> dict:
    streams_of = jax.random.split(jax.random.key(seed), 8)
    own_keys = jax.random.split(jax.random.fold_in(streams_of[7], part), 8)
    return {
        "tokens": bell_draw(own_keys[0], (TOKENS, D), 1.0, 6.0, ((0, 4), (1, 4))),
        "gate_weight": bell_draw(streams_of[1], (D, FF), (D // 2) ** -0.5, 0.09375, ((0, 4), (1, 4))),
        "up_weight": bell_draw(streams_of[2], (D, FF), (D // 2) ** -0.5, 0.09375, ((0, 4), (1, 4))),
        "down_weight": bell_draw(streams_of[3], (FF, D), (FF // 2) ** -0.5, 0.0625, ((0, 4), (1, 4))),
        "gate_keep": draw_gate_keep(jax.random.fold_in(streams_of[7], 71), part),
        "up_keep": draw_up_keep(jax.random.fold_in(streams_of[7], 71), part),
        "down_keep": draw_down_keep(jax.random.fold_in(streams_of[7], 71), part),
    }


def widen(keep_mask):
    spread = jnp.repeat(jnp.repeat(keep_mask, BLOCK, axis=0), BLOCK, axis=1)
    return spread.astype(jnp.bfloat16)


def slab_sum(left, right, pieces):
    span = right.shape[0] // pieces

    def add_slab(index, total):
        start = (index * span).astype(jnp.int32)
        left_slab = lax.dynamic_slice_in_dim(left, start, span, 1)
        right_slab = lax.dynamic_slice_in_dim(right, start, span, 0)
        term = jnp.dot(left_slab, right_slab, preferred_element_type=jnp.float32).astype(jnp.bfloat16)
        term = lax.optimization_barrier(term)
        return total + term.astype(jnp.float32)

    empty = jnp.zeros((left.shape[0], right.shape[1]), jnp.float32)
    return lax.fori_loop(0, pieces, add_slab, empty)


def reference(tokens, gate_weight, up_weight, down_weight, gate_keep, up_keep, down_keep):
    gate = slab_sum(tokens, gate_weight * widen(gate_keep), N_NARROW)
    up = slab_sum(tokens, up_weight * widen(up_keep), N_NARROW)
    hidden = (jax.nn.silu(gate) * up).astype(jnp.bfloat16)
    mixed = slab_sum(hidden, down_weight * widen(down_keep), N_WIDE)
    return mixed.astype(jnp.bfloat16)
```

```python
import jax
import jax.numpy as jnp
from jax import lax
from jax.experimental import pallas as pl
from jax.experimental.pallas import tpu as pltpu
from jax.sharding import PartitionSpec as P

BLOCK = 128
MESH = pl.DeviceIdType.MESH
CHUNK = 512
PIECE = 512
VMEM_LIMIT = 62 * 1024 * 1024


def widen(keep_mask):
    rows, cols = keep_mask.shape
    spread = jnp.broadcast_to(keep_mask[:, None, :, None], (rows, BLOCK, cols, BLOCK))
    return spread.reshape(rows * BLOCK, cols * BLOCK).astype(jnp.bfloat16)


def general_body(tokens, gate_weight, up_weight, down_weight, gate_keep, up_keep, down_keep):
    columns = gate_weight.shape[1]
    both_eff = jnp.concatenate((gate_weight * widen(gate_keep), up_weight * widen(up_keep)), axis=1)
    down_eff = down_weight * widen(down_keep)
    partial_value = jnp.dot(
        lax.all_gather(tokens, "wide", axis=0, tiled=True),
        both_eff,
        preferred_element_type=jnp.float32,
    )
    summed = lax.psum_scatter(
        partial_value.astype(jnp.bfloat16), "narrow", scatter_dimension=0, tiled=True
    ).astype(jnp.float32)
    share_rows = (jax.nn.silu(summed[:, :columns]) * summed[:, columns:]).astype(jnp.bfloat16)
    hidden = lax.all_gather(share_rows, "narrow", axis=0, tiled=True)
    return lax.psum_scatter(
        jnp.dot(hidden, down_eff, preferred_element_type=jnp.float32).astype(jnp.bfloat16),
        "wide",
        scatter_dimension=0,
        tiled=True,
    )


def spread_columns(keep):
    blocks = keep.shape[1]
    shape = (blocks, blocks * BLOCK)
    row = lax.broadcasted_iota(jnp.int32, shape, 0)
    col = lax.broadcasted_iota(jnp.int32, shape, 1)
    low = row * BLOCK
    pick = jnp.where((col >= low) & (col < low + BLOCK), 1.0, 0.0).astype(jnp.bfloat16)
    return jnp.dot(keep.astype(jnp.bfloat16), pick, preferred_element_type=jnp.float32)


def make_kernel(rows, n_wide, depth, ff, chunks):
    share = rows

    def kernel(tok, gate, up, down, gkeep, ukeep, dkeep, out,
               tokall, gbuf, ubuf, dbuf, gmask, umask, dmask,
               pbuf, sibs, sibr, own, xs, xr, hid, acc, zs, zr,
               t_s, t_r, w_g, w_u, w_d, sib_s, sib_r, x_s, x_r,
               hs_s, hs_r, hx_s, hx_r, hf_s, hf_r, z_s, z_r):
        w = lax.axis_index("wide")
        n = lax.axis_index("narrow")
        x = n // 2
        k = n % 2
        sib = 2 * x + (1 - k)
        peer = 2 * (1 - x) + k
        diag = 2 * (1 - x) + (1 - k)

        def load_gate(c):
            return pltpu.make_async_copy(gate.at[:, pl.ds(pl.multiple_of(c * CHUNK, CHUNK), CHUNK)], gbuf.at[c], w_g.at[c])

        def load_up(c):
            return pltpu.make_async_copy(up.at[:, pl.ds(pl.multiple_of(c * CHUNK, CHUNK), CHUNK)], ubuf.at[c], w_u.at[c])

        def load_down(c):
            return pltpu.make_async_copy(down.at[pl.ds(pl.multiple_of(c * CHUNK, CHUNK), CHUNK), :], dbuf.at[c], w_d.at[c])

        @pl.loop(0, chunks)
        def _(c):
            load_gate(c).start()
            load_up(c).start()

        barrier = pltpu.get_barrier_semaphore()
        for d in range(1, n_wide):
            pl.semaphore_signal(barrier, inc=1, device_id={"wide": (w + d) % n_wide}, device_id_type=MESH)
        for other in (sib, peer):
            pl.semaphore_signal(barrier, inc=1, device_id={"narrow": other}, device_id_type=MESH)
        pl.semaphore_wait(barrier, n_wide + 1)

        def token_copy(d):
            return pltpu.make_async_remote_copy(
                src_ref=tok, dst_ref=tokall.at[pl.ds(pl.multiple_of(w * rows, rows), rows), :],
                send_sem=t_s.at[d - 1], recv_sem=t_r.at[d - 1],
                device_id={"wide": (w + d) % n_wide}, device_id_type=MESH)

        def token_arrival(d):
            source = (w + n_wide - d) % n_wide
            return pltpu.make_async_remote_copy(
                src_ref=tok, dst_ref=tokall.at[pl.ds(pl.multiple_of(source * rows, rows), rows), :],
                send_sem=t_s.at[d - 1], recv_sem=t_r.at[d - 1],
                device_id={"wide": (w + d) % n_wide}, device_id_type=MESH)

        for d in (2, 3, 1):
            token_copy(d).start()
        tokall[pl.ds(pl.multiple_of(w * rows, rows), rows), :] = tok[...]

        gmask[...] = spread_columns(gkeep[...])
        umask[...] = spread_columns(ukeep[...])
        dmask[...] = spread_columns(dkeep[...])
        acc[...] = jnp.zeros_like(acc)

        def apply_rows(buf, c, mask, mask_row, cols, width, row0):
            line = mask[pl.ds(mask_row, 1), cols]
            line = jnp.broadcast_to(line, (BLOCK, width)).astype(jnp.bfloat16)
            at = pl.ds(row0, BLOCK)
            buf[c, at, :] = buf[c, at, :] * line

        def mask_gate_up(c):
            cols = pl.ds(pl.multiple_of(c * CHUNK, CHUNK), CHUNK)

            @pl.loop(0, depth // BLOCK)
            def _(b):
                row0 = pl.multiple_of(b * BLOCK, BLOCK)
                apply_rows(gbuf, c, gmask, b, cols, CHUNK, row0)
                apply_rows(ubuf, c, umask, b, cols, CHUNK, row0)

        def mask_down(c):
            for b in range(CHUNK // BLOCK):
                apply_rows(dbuf, c, dmask, c * (CHUNK // BLOCK) + b, slice(None), depth, b * BLOCK)

        @pl.loop(0, chunks)
        def _(c):
            load_gate(c).wait()
            load_up(c).wait()
            load_down(c).start()
            mask_gate_up(c)

        for d in (1, 2, 3):
            token_arrival(d).wait_recv()

        def remote(src, dst, send, recv, other):
            return pltpu.make_async_remote_copy(
                src_ref=src, dst_ref=dst, send_sem=send, recv_sem=recv,
                device_id={"narrow": other}, device_id_type=MESH)

        def sib_copy(c):
            return remote(sibs.at[c], sibr.at[c], sib_s.at[c], sib_r.at[c], sib)

        def x_copy(c):
            return remote(xs.at[c], xr.at[c], x_s.at[c], x_r.at[c], peer)

        def hid_sib(c, which):
            return remote(hid.at[c, which], hid.at[c, which], hs_s.at[c], hs_r.at[c], sib)

        def hid_x(c, which):
            return remote(hid.at[c, which], hid.at[c, which], hx_s.at[c], hx_r.at[c], peer)

        def hid_forward(c, which):
            return remote(hid.at[c, which], hid.at[c, which], hf_s.at[c], hf_r.at[c], sib)

        def share_at(j):
            return pl.ds(pl.multiple_of(j * share, share), share)

        def stage_partial(c):
            slot = c % 2
            all_tokens = tokall[...]
            pbuf[slot, :, 0:CHUNK] = jnp.dot(all_tokens, gbuf[c], preferred_element_type=jnp.float32)
            pbuf[slot, :, CHUNK:] = jnp.dot(all_tokens, ubuf[c], preferred_element_type=jnp.float32)
            for side in range(2):
                sibs[c, side] = pbuf[slot, share_at(2 * side + 1 - k), :].astype(jnp.bfloat16)
            sib_copy(c).start()

        def stage_chip_sum(c):
            slot = c % 2
            sib_copy(c).wait_recv()
            xs[c] = (pbuf[slot, share_at(peer), :] + sibr[c, 1 - x].astype(jnp.float32)).astype(jnp.bfloat16)
            x_copy(c).start()
            own[c] = pbuf[slot, share_at(n), :] + sibr[c, x].astype(jnp.float32)

        def stage_hidden(c):
            x_copy(c).wait_recv()
            both = own[c] + xr[c].astype(jnp.float32)
            g, u = both[:, :CHUNK], both[:, CHUNK:]
            hid[c, n] = (g / (1.0 + jnp.exp(-g)) * u).astype(jnp.bfloat16)
            hid_x(c, n).start()
            hid_sib(c, n).start()

        def stage_forward(c):
            hid_x(c, peer).wait_recv()
            hid_forward(c, peer).start()

        def wait_hidden(c):
            hid_sib(c, sib).wait_recv()
            hid_forward(c, diag).wait_recv()

        def stage_down(c):
            wait_hidden(c)
            h = hid[c].reshape(4 * share, CHUNK)

            @pl.loop(0, depth // PIECE)
            def _(q):
                cols = pl.ds(pl.multiple_of(q * PIECE, PIECE), PIECE)
                acc[:, cols] += jnp.dot(h, dbuf[c, :, cols], preferred_element_type=jnp.float32)

        @pl.loop(0, chunks + 5)
        def _(t):
            @pl.when(t < chunks)
            def _():
                stage_partial(t)

            @pl.when((t >= 1) & (t < chunks + 1))
            def _():
                stage_chip_sum(t - 1)

            @pl.when(t < chunks)
            def _():
                load_down(t).wait()
                mask_down(t)

            @pl.when((t >= 3) & (t < chunks + 3))
            def _():
                stage_hidden(t - 3)

            @pl.when((t >= 4) & (t < chunks + 4))
            def _():
                stage_forward(t - 4)

            @pl.when((t >= 5) & (t < chunks + 4))
            def _():
                stage_down(t - 5)

        def z_copy(q, d):
            return pltpu.make_async_remote_copy(
                src_ref=zs.at[q, d - 1], dst_ref=zr.at[q, d - 1],
                send_sem=z_s.at[q, d - 1], recv_sem=z_r.at[q, d - 1],
                device_id={"wide": (w + d) % n_wide}, device_id_type=MESH)

        wait_hidden(chunks - 1)
        last = hid[chunks - 1].reshape(4 * share, CHUNK)

        @pl.loop(0, depth // PIECE)
        def _(q):
            cols = pl.ds(pl.multiple_of(q * PIECE, PIECE), PIECE)
            acc[:, cols] += jnp.dot(last, dbuf[chunks - 1, :, cols], preferred_element_type=jnp.float32)
            for d in (2, 3, 1):
                zs[q, d - 1] = acc[share_at((w + d) % n_wide), cols].astype(jnp.bfloat16)
                z_copy(q, d).start()

        @pl.loop(0, depth // PIECE)
        def _(q):
            cols = pl.ds(pl.multiple_of(q * PIECE, PIECE), PIECE)
            total = acc[share_at(w), cols]
            for d in (1, 2, 3):
                z_copy(q, d).wait_recv()
                total = total + zr[q, d - 1].astype(jnp.float32)
            out[:, cols] = total.astype(jnp.bfloat16)

        for d in (1, 2, 3):
            token_copy(d).wait_send()

        @pl.loop(0, chunks)
        def _(c):
            sib_copy(c).wait_send()
            x_copy(c).wait_send()
            hid_x(c, n).wait_send()
            hid_sib(c, n).wait_send()
            hid_forward(c, peer).wait_send()

        @pl.loop(0, depth // PIECE)
        def _(q):
            for d in (1, 2, 3):
                z_copy(q, d).wait_send()

    return kernel


def fused_body(n_wide):
    def body(tokens, gate_weight, up_weight, down_weight, gate_keep, up_keep, down_keep):
        rows, depth = tokens.shape
        ff = gate_weight.shape[1]
        chunks = ff // CHUNK
        pieces = depth // PIECE
        bf, f32 = jnp.bfloat16, jnp.float32
        vmem = pl.BlockSpec(memory_space=pltpu.VMEM)
        anywhere = pl.BlockSpec(memory_space=pl.ANY)
        dma = pltpu.SemaphoreType.DMA
        return pl.pallas_call(
            make_kernel(rows, n_wide, depth, ff, chunks),
            out_shape=jax.ShapeDtypeStruct((rows, depth), bf),
            in_specs=[vmem, anywhere, anywhere, anywhere, vmem, vmem, vmem],
            out_specs=vmem,
            scratch_shapes=[
                pltpu.VMEM((n_wide * rows, depth), bf),
                pltpu.VMEM((chunks, depth, CHUNK), bf),
                pltpu.VMEM((chunks, depth, CHUNK), bf),
                pltpu.VMEM((chunks, CHUNK, depth), bf),
                pltpu.VMEM((depth // BLOCK, ff), f32),
                pltpu.VMEM((depth // BLOCK, ff), f32),
                pltpu.VMEM((ff // BLOCK, depth), f32),
                pltpu.VMEM((2, n_wide * rows, 2 * CHUNK), f32),
                pltpu.VMEM((chunks, 2, rows, 2 * CHUNK), bf),
                pltpu.VMEM((chunks, 2, rows, 2 * CHUNK), bf),
                pltpu.VMEM((chunks, rows, 2 * CHUNK), f32),
                pltpu.VMEM((chunks, rows, 2 * CHUNK), bf),
                pltpu.VMEM((chunks, rows, 2 * CHUNK), bf),
                pltpu.VMEM((chunks, 4, rows, CHUNK), bf),
                pltpu.VMEM((n_wide * rows, depth), f32),
                pltpu.VMEM((pieces, n_wide - 1, rows, PIECE), bf),
                pltpu.VMEM((pieces, n_wide - 1, rows, PIECE), bf),
                dma((n_wide - 1,)), dma((n_wide - 1,)),
                dma((chunks,)), dma((chunks,)), dma((chunks,)),
                dma((chunks,)), dma((chunks,)), dma((chunks,)), dma((chunks,)),
                dma((chunks,)), dma((chunks,)), dma((chunks,)), dma((chunks,)),
                dma((chunks,)), dma((chunks,)),
                dma((pieces, n_wide - 1)), dma((pieces, n_wide - 1)),
            ],
            compiler_params=pltpu.CompilerParams(
                collective_id=0, has_side_effects=True, vmem_limit_bytes=VMEM_LIMIT),
        )(tokens, gate_weight, up_weight, down_weight, gate_keep, up_keep, down_keep)

    return body


def solution(mesh):
    in_specs = (
        P(("groups", "wide"), "narrow"),
        P("narrow", "wide"),
        P("narrow", "wide"),
        P("wide", "narrow"),
        P("narrow", "wide"),
        P("narrow", "wide"),
        P("wide", "narrow"),
    )
    out_specs = P(("groups", "wide"), "narrow")
    fits = mesh.shape["wide"] == 4 and mesh.shape["narrow"] == 4
    body = fused_body(mesh.shape["wide"]) if fits else general_body
    return jax.shard_map(body, mesh=mesh, in_specs=in_specs, out_specs=out_specs, check_vma=False)
```

```python
import jax
import jax.numpy as jnp
from jax import lax
from jax.experimental import pallas as pl
from jax.experimental.pallas import tpu as pltpu
from jax.sharding import PartitionSpec as P

BLOCK = 128
MESH = pl.DeviceIdType.MESH
CHUNK = 512
PIECE = 1024
HALVES = 1
SLOTS = 3
AHEAD = 3
INFLIGHT = 3
SUM_LAG = 2
HIDDEN_LAG = 5
FORWARD = 2
EXTRA = 0
VMEM_LIMIT = 62 * 1024 * 1024


def widen(keep_mask):
    rows, cols = keep_mask.shape
    spread = jnp.broadcast_to(keep_mask[:, None, :, None], (rows, BLOCK, cols, BLOCK))
    return spread.reshape(rows * BLOCK, cols * BLOCK).astype(jnp.bfloat16)


def general_body(tokens, gate_weight, up_weight, down_weight, gate_keep, up_keep, down_keep):
    columns = gate_weight.shape[1]
    both_eff = jnp.concatenate((gate_weight * widen(gate_keep), up_weight * widen(up_keep)), axis=1)
    down_eff = down_weight * widen(down_keep)
    partial_value = jnp.dot(
        lax.all_gather(tokens, "wide", axis=0, tiled=True),
        both_eff,
        preferred_element_type=jnp.float32,
    )
    summed = lax.psum_scatter(
        partial_value.astype(jnp.bfloat16), "narrow", scatter_dimension=0, tiled=True
    ).astype(jnp.float32)
    share_rows = (jax.nn.silu(summed[:, :columns]) * summed[:, columns:]).astype(jnp.bfloat16)
    hidden = lax.all_gather(share_rows, "narrow", axis=0, tiled=True)
    return lax.psum_scatter(
        jnp.dot(hidden, down_eff, preferred_element_type=jnp.float32).astype(jnp.bfloat16),
        "wide",
        scatter_dimension=0,
        tiled=True,
    )


def spread_columns(keep):
    blocks = keep.shape[1]
    shape = (blocks, blocks * BLOCK)
    row = lax.broadcasted_iota(jnp.int32, shape, 0)
    col = lax.broadcasted_iota(jnp.int32, shape, 1)
    low = row * BLOCK
    pick = jnp.where((col >= low) & (col < low + BLOCK), 1.0, 0.0).astype(jnp.bfloat16)
    return jnp.dot(keep.astype(jnp.bfloat16), pick, preferred_element_type=jnp.float32)


def make_kernel(rows, n_wide, depth, ff, chunks):
    share = rows // HALVES

    def kernel(tok, gate, up, down, gkeep, ukeep, dkeep, out,
               tokall, gbuf, ubuf, dbuf, gmask, umask, dmask,
               pbuf, sibs, sibr, own, xs, xr, hid, acc, zs, zr,
               t_s, t_r, w_g, w_u, w_d, sib_s, sib_r, x_s, x_r,
               hs_s, hs_r, hx_s, hx_r, hf_s, hf_r, z_s, z_r):
        w = lax.axis_index("wide")
        n = lax.axis_index("narrow")
        x = n // 2
        k = n % 2
        sib = 2 * x + (1 - k)
        peer = 2 * (1 - x) + k
        diag = 2 * (1 - x) + (1 - k)

        def load_gate(c):
            return pltpu.make_async_copy(gate.at[:, pl.ds(pl.multiple_of(c * CHUNK, CHUNK), CHUNK)], gbuf.at[c], w_g.at[c])

        def load_up(c):
            return pltpu.make_async_copy(up.at[:, pl.ds(pl.multiple_of(c * CHUNK, CHUNK), CHUNK)], ubuf.at[c], w_u.at[c])

        def load_down(c):
            return pltpu.make_async_copy(down.at[pl.ds(pl.multiple_of(c * CHUNK, CHUNK), CHUNK), :], dbuf.at[c], w_d.at[c])

        def start_load(item):
            @pl.when(item < chunks)
            def _():
                load_gate(item).start()
                load_up(item).start()

            @pl.when((item >= chunks) & (item < 2 * chunks))
            def _():
                load_down(item - chunks).start()

        @pl.loop(0, INFLIGHT)
        def _(item):
            start_load(item)

        barrier = pltpu.get_barrier_semaphore()
        for d in range(1, n_wide):
            pl.semaphore_signal(barrier, inc=1, device_id={"wide": (w + d) % n_wide}, device_id_type=MESH)
        for other in (sib, peer):
            pl.semaphore_signal(barrier, inc=1, device_id={"narrow": other}, device_id_type=MESH)
        pl.semaphore_wait(barrier, n_wide + 1)

        def token_move(h, d, owner):
            return pltpu.make_async_remote_copy(
                src_ref=tok.at[pl.ds(h * share, share), :],
                dst_ref=tokall.at[h, pl.ds(pl.multiple_of(owner * share, share), share), :],
                send_sem=t_s.at[h, d - 1], recv_sem=t_r.at[h, d - 1],
                device_id={"wide": (w + d) % n_wide}, device_id_type=MESH)

        def token_copy(h, d):
            return token_move(h, d, w)

        def token_arrival(h, d):
            return token_move(h, d, (w + n_wide - d) % n_wide)

        for d in (2, 3, 1):
            token_copy(0, d).start()
        for h in range(HALVES):
            tokall[h, pl.ds(pl.multiple_of(w * share, share), share), :] = tok[h * share:(h + 1) * share, :]

        gmask[...] = spread_columns(gkeep[...])
        umask[...] = spread_columns(ukeep[...])
        dmask[...] = spread_columns(dkeep[...])
        acc[...] = jnp.zeros_like(acc)

        def apply_rows(buf, c, mask, mask_row, cols, width, row0):
            line = mask[pl.ds(mask_row, 1), cols]
            line = jnp.broadcast_to(line, (BLOCK, width)).astype(jnp.bfloat16)
            at = pl.ds(row0, BLOCK)
            buf[c, at, :] = buf[c, at, :] * line

        def prepare_gate_up(c):
            load_gate(c).wait()
            load_up(c).wait()
            start_load(c + INFLIGHT)
            cols = pl.ds(pl.multiple_of(c * CHUNK, CHUNK), CHUNK)

            @pl.loop(0, depth // BLOCK)
            def _(b):
                row0 = pl.multiple_of(b * BLOCK, BLOCK)
                apply_rows(gbuf, c, gmask, b, cols, CHUNK, row0)
                apply_rows(ubuf, c, umask, b, cols, CHUNK, row0)

        def prepare_down(c):
            load_down(c).wait()
            start_load(chunks + c + INFLIGHT)
            for b in range(CHUNK // BLOCK):
                apply_rows(dbuf, c, dmask, c * (CHUNK // BLOCK) + b, slice(None), depth, b * BLOCK)

        @pl.loop(0, AHEAD)
        def _(c):
            prepare_gate_up(c)

        for d in (1, 2, 3):
            token_arrival(0, d).wait_recv()
        def remote(src, dst, send, recv, other):
            return pltpu.make_async_remote_copy(
                src_ref=src, dst_ref=dst, send_sem=send, recv_sem=recv,
                device_id={"narrow": other}, device_id_type=MESH)

        def sib_copy(v):
            return remote(sibs.at[v], sibr.at[v], sib_s.at[v], sib_r.at[v], sib)

        def x_copy(v):
            return remote(xs.at[v], xr.at[v], x_s.at[v], x_r.at[v], peer)

        def hid_sib(v, which):
            return remote(hid.at[v, which], hid.at[v, which], hs_s.at[v], hs_r.at[v], sib)

        def hid_x(v, which):
            return remote(hid.at[v, which], hid.at[v, which], hx_s.at[v], hx_r.at[v], peer)

        def hid_forward(v, which):
            return remote(hid.at[v, which], hid.at[v, which], hf_s.at[v], hf_r.at[v], sib)

        def share_at(j):
            return pl.ds(pl.multiple_of(j * share, share), share)

        units = HALVES * chunks

        def stage_partial(v):
            slot = v % SLOTS
            h, c = v // chunks, v % chunks
            half_tokens = tokall[h]
            pbuf[slot, :, 0:CHUNK] = jnp.dot(half_tokens, gbuf[c], preferred_element_type=jnp.float32)
            pbuf[slot, :, CHUNK:] = jnp.dot(half_tokens, ubuf[c], preferred_element_type=jnp.float32)
            for side in range(2):
                sibs[v, side] = pbuf[slot, share_at(2 * side + 1 - k), :].astype(jnp.bfloat16)
            sib_copy(v).start()

        def stage_chip_sum(v):
            slot = v % SLOTS
            sib_copy(v).wait_recv()
            xs[v] = (pbuf[slot, share_at(peer), :] + sibr[v, 1 - x].astype(jnp.float32)).astype(jnp.bfloat16)
            x_copy(v).start()
            own[v] = pbuf[slot, share_at(n), :] + sibr[v, x].astype(jnp.float32)

        def stage_hidden(v):
            x_copy(v).wait_recv()
            both = own[v] + xr[v].astype(jnp.float32)
            g, u = both[:, :CHUNK], both[:, CHUNK:]
            hid[v, n] = (g / (1.0 + jnp.exp(-g)) * u).astype(jnp.bfloat16)
            hid_x(v, n).start()
            hid_sib(v, n).start()

        def stage_forward(v):
            hid_x(v, peer).wait_recv()
            hid_forward(v, peer).start()

        def z_copy(h, q, d):
            return pltpu.make_async_remote_copy(
                src_ref=zs.at[h, q, d - 1], dst_ref=zr.at[h, q, d - 1],
                send_sem=z_s.at[h, q, d - 1], recv_sem=z_r.at[h, q, d - 1],
                device_id={"wide": (w + d) % n_wide}, device_id_type=MESH)

        def stage_down(v):
            h, c = v // chunks, v % chunks

            hid_sib(v, sib).wait_recv()
            hid_forward(v, diag).wait_recv()

            @pl.loop(0, depth // PIECE)
            def _(q):
                cols = pl.ds(pl.multiple_of(q * PIECE, PIECE), PIECE)
                hidden = hid[v].reshape(n_wide * share, CHUNK)
                acc[h, :, cols] += jnp.dot(hidden, dbuf[c, :, cols], preferred_element_type=jnp.float32)

                @pl.when(c == chunks - 1)
                def _():
                    for d in (2, 3, 1):
                        zs[h, q, d - 1] = acc[h, share_at((w + d) % n_wide), cols].astype(jnp.bfloat16)
                        z_copy(h, q, d).start()

        def staged(t, lag, stage):
            @pl.when((t >= lag) & (t < chunks + lag))
            def _():
                stage(t - lag)

        @pl.loop(0, 2 * chunks + EXTRA)
        def _(t):
            @pl.when((t >= AHEAD) & (t < chunks))
            def _():
                prepare_gate_up(t)

            staged(t, 0, stage_partial)

            @pl.when((t >= chunks) & (t < 2 * chunks))
            def _():
                prepare_down(t - chunks)

            staged(t, SUM_LAG, stage_chip_sum)
            staged(t, HIDDEN_LAG, stage_hidden)
            staged(t, HIDDEN_LAG + FORWARD, stage_forward)
            staged(t, chunks + EXTRA, stage_down)

        for h in range(HALVES):
            rows_at = pl.ds(h * share, share)

            @pl.loop(0, depth // PIECE)
            def _(q):
                cols = pl.ds(pl.multiple_of(q * PIECE, PIECE), PIECE)
                total = acc[h, share_at(w), cols]
                for d in (1, 2, 3):
                    z_copy(h, q, d).wait_recv()
                    total = total + zr[h, q, d - 1].astype(jnp.float32)
                out[rows_at, cols] = total.astype(jnp.bfloat16)

        for h in range(HALVES):
            for d in (1, 2, 3):
                token_copy(h, d).wait_send()

        @pl.loop(0, units)
        def _(v):
            sib_copy(v).wait_send()
            x_copy(v).wait_send()
            hid_x(v, n).wait_send()
            hid_sib(v, n).wait_send()
            hid_forward(v, peer).wait_send()

        for h in range(HALVES):
            @pl.loop(0, depth // PIECE)
            def _(q):
                for d in (1, 2, 3):
                    z_copy(h, q, d).wait_send()

    return kernel


def fused_body(n_wide):
    def body(tokens, gate_weight, up_weight, down_weight, gate_keep, up_keep, down_keep):
        rows, depth = tokens.shape
        ff = gate_weight.shape[1]
        chunks = ff // CHUNK
        pieces = depth // PIECE
        share = rows // HALVES
        units = HALVES * chunks
        bf, f32 = jnp.bfloat16, jnp.float32
        vmem = pl.BlockSpec(memory_space=pltpu.VMEM)
        anywhere = pl.BlockSpec(memory_space=pl.ANY)
        dma = pltpu.SemaphoreType.DMA
        return pl.pallas_call(
            make_kernel(rows, n_wide, depth, ff, chunks),
            out_shape=jax.ShapeDtypeStruct((rows, depth), bf),
            in_specs=[vmem, anywhere, anywhere, anywhere, vmem, vmem, vmem],
            out_specs=vmem,
            scratch_shapes=[
                pltpu.VMEM((HALVES, n_wide * share, depth), bf),
                pltpu.VMEM((chunks, depth, CHUNK), bf),
                pltpu.VMEM((chunks, depth, CHUNK), bf),
                pltpu.VMEM((chunks, CHUNK, depth), bf),
                pltpu.VMEM((depth // BLOCK, ff), f32),
                pltpu.VMEM((depth // BLOCK, ff), f32),
                pltpu.VMEM((ff // BLOCK, depth), f32),
                pltpu.VMEM((SLOTS, n_wide * share, 2 * CHUNK), f32),
                pltpu.VMEM((units, 2, share, 2 * CHUNK), bf),
                pltpu.VMEM((units, 2, share, 2 * CHUNK), bf),
                pltpu.VMEM((units, share, 2 * CHUNK), f32),
                pltpu.VMEM((units, share, 2 * CHUNK), bf),
                pltpu.VMEM((units, share, 2 * CHUNK), bf),
                pltpu.VMEM((units, 4, share, CHUNK), bf),
                pltpu.VMEM((HALVES, n_wide * share, depth), f32),
                pltpu.VMEM((HALVES, pieces, n_wide - 1, share, PIECE), bf),
                pltpu.VMEM((HALVES, pieces, n_wide - 1, share, PIECE), bf),
                dma((HALVES, n_wide - 1)), dma((HALVES, n_wide - 1)),
                dma((chunks,)), dma((chunks,)), dma((chunks,)),
                dma((units,)), dma((units,)), dma((units,)), dma((units,)),
                dma((units,)), dma((units,)), dma((units,)), dma((units,)),
                dma((units,)), dma((units,)),
                dma((HALVES, pieces, n_wide - 1)), dma((HALVES, pieces, n_wide - 1)),
            ],
            compiler_params=pltpu.CompilerParams(
                collective_id=0, has_side_effects=True, vmem_limit_bytes=VMEM_LIMIT),
        )(tokens, gate_weight, up_weight, down_weight, gate_keep, up_keep, down_keep)

    return body


def solution(mesh):
    in_specs = (
        P(("groups", "wide"), "narrow"),
        P("narrow", "wide"),
        P("narrow", "wide"),
        P("wide", "narrow"),
        P("narrow", "wide"),
        P("narrow", "wide"),
        P("wide", "narrow"),
    )
    out_specs = P(("groups", "wide"), "narrow")
    fits = mesh.shape["wide"] == 4 and mesh.shape["narrow"] == 4
    body = fused_body(mesh.shape["wide"]) if fits else general_body
    return jax.shard_map(body, mesh=mesh, in_specs=in_specs, out_specs=out_specs, check_vma=False)
```

```python
import jax
import jax.numpy as jnp
from jax import lax
from jax.experimental import pallas as pl
from jax.experimental.pallas import tpu as pltpu
from jax.sharding import PartitionSpec as P

BLOCK = 128
MESH = pl.DeviceIdType.MESH
CHUNK = 512
PIECE = 1024
HALVES = 1
SLOTS = 3
AHEAD = 3
INFLIGHT = 3
SUM_LAG = 2
HIDDEN_LAG = 5
FORWARD = 3
EXTRA = 1
VMEM_LIMIT = 62 * 1024 * 1024


def widen(keep_mask):
    rows, cols = keep_mask.shape
    spread = jnp.broadcast_to(keep_mask[:, None, :, None], (rows, BLOCK, cols, BLOCK))
    return spread.reshape(rows * BLOCK, cols * BLOCK).astype(jnp.bfloat16)


def general_body(tokens, gate_weight, up_weight, down_weight, gate_keep, up_keep, down_keep):
    columns = gate_weight.shape[1]
    both_eff = jnp.concatenate((gate_weight * widen(gate_keep), up_weight * widen(up_keep)), axis=1)
    down_eff = down_weight * widen(down_keep)
    partial_value = jnp.dot(
        lax.all_gather(tokens, "wide", axis=0, tiled=True),
        both_eff,
        preferred_element_type=jnp.float32,
    )
    summed = lax.psum_scatter(
        partial_value.astype(jnp.bfloat16), "narrow", scatter_dimension=0, tiled=True
    ).astype(jnp.float32)
    share_rows = (jax.nn.silu(summed[:, :columns]) * summed[:, columns:]).astype(jnp.bfloat16)
    hidden = lax.all_gather(share_rows, "narrow", axis=0, tiled=True)
    return lax.psum_scatter(
        jnp.dot(hidden, down_eff, preferred_element_type=jnp.float32).astype(jnp.bfloat16),
        "wide",
        scatter_dimension=0,
        tiled=True,
    )


def spread_columns(keep):
    blocks = keep.shape[1]
    shape = (blocks, blocks * BLOCK)
    row = lax.broadcasted_iota(jnp.int32, shape, 0)
    col = lax.broadcasted_iota(jnp.int32, shape, 1)
    low = row * BLOCK
    pick = jnp.where((col >= low) & (col < low + BLOCK), 1.0, 0.0).astype(jnp.bfloat16)
    return jnp.dot(keep.astype(jnp.bfloat16), pick, preferred_element_type=jnp.float32)


def make_kernel(rows, n_wide, depth, ff, chunks):
    share = rows // HALVES

    def kernel(tok, gate, up, down, gkeep, ukeep, dkeep, out,
               tokall, gbuf, ubuf, dbuf, gmask, umask, dmask,
               pbuf, sibs, sibr, own, xs, xr, hid, acc, zs, zr,
               t_s, t_r, w_g, w_u, w_d, sib_s, sib_r, x_s, x_r,
               hs_s, hs_r, hx_s, hx_r, hf_s, hf_r, z_s, z_r):
        w = lax.axis_index("wide")
        n = lax.axis_index("narrow")
        x = n // 2
        k = n % 2
        sib = 2 * x + (1 - k)
        peer = 2 * (1 - x) + k
        diag = 2 * (1 - x) + (1 - k)

        def load_gate(c):
            return pltpu.make_async_copy(gate.at[:, pl.ds(pl.multiple_of(c * CHUNK, CHUNK), CHUNK)], gbuf.at[c], w_g.at[c])

        def load_up(c):
            return pltpu.make_async_copy(up.at[:, pl.ds(pl.multiple_of(c * CHUNK, CHUNK), CHUNK)], ubuf.at[c], w_u.at[c])

        def load_down(c):
            return pltpu.make_async_copy(down.at[pl.ds(pl.multiple_of(c * CHUNK, CHUNK), CHUNK), :], dbuf.at[c], w_d.at[c])

        def start_load(item):
            @pl.when(item < chunks)
            def _():
                load_gate(item).start()
                load_up(item).start()

            @pl.when((item >= chunks) & (item < 2 * chunks))
            def _():
                load_down(item - chunks).start()

        @pl.loop(0, INFLIGHT)
        def _(item):
            start_load(item)

        barrier = pltpu.get_barrier_semaphore()
        for d in range(1, n_wide):
            pl.semaphore_signal(barrier, inc=1, device_id={"wide": (w + d) % n_wide}, device_id_type=MESH)
        for other in (sib, peer):
            pl.semaphore_signal(barrier, inc=1, device_id={"narrow": other}, device_id_type=MESH)
        pl.semaphore_wait(barrier, n_wide + 1)

        def token_move(h, d, owner):
            return pltpu.make_async_remote_copy(
                src_ref=tok.at[pl.ds(h * share, share), :],
                dst_ref=tokall.at[h, pl.ds(pl.multiple_of(owner * share, share), share), :],
                send_sem=t_s.at[h, d - 1], recv_sem=t_r.at[h, d - 1],
                device_id={"wide": (w + d) % n_wide}, device_id_type=MESH)

        def token_copy(h, d):
            return token_move(h, d, w)

        def token_arrival(h, d):
            return token_move(h, d, (w + n_wide - d) % n_wide)

        for d in (2, 3, 1):
            token_copy(0, d).start()
        for h in range(HALVES):
            tokall[h, pl.ds(pl.multiple_of(w * share, share), share), :] = tok[h * share:(h + 1) * share, :]

        gmask[...] = spread_columns(gkeep[...])
        umask[...] = spread_columns(ukeep[...])
        dmask[...] = spread_columns(dkeep[...])
        acc[...] = jnp.zeros_like(acc)

        def apply_rows(buf, c, mask, mask_row, cols, width, row0):
            line = mask[pl.ds(mask_row, 1), cols]
            line = jnp.broadcast_to(line, (BLOCK, width)).astype(jnp.bfloat16)
            at = pl.ds(row0, BLOCK)
            buf[c, at, :] = buf[c, at, :] * line

        def prepare_gate_up(c):
            load_gate(c).wait()
            load_up(c).wait()
            start_load(c + INFLIGHT)
            cols = pl.ds(pl.multiple_of(c * CHUNK, CHUNK), CHUNK)

            @pl.loop(0, depth // BLOCK)
            def _(b):
                row0 = pl.multiple_of(b * BLOCK, BLOCK)
                apply_rows(gbuf, c, gmask, b, cols, CHUNK, row0)
                apply_rows(ubuf, c, umask, b, cols, CHUNK, row0)

        def prepare_down(c):
            load_down(c).wait()
            start_load(chunks + c + INFLIGHT)
            for b in range(CHUNK // BLOCK):
                apply_rows(dbuf, c, dmask, c * (CHUNK // BLOCK) + b, slice(None), depth, b * BLOCK)

        @pl.loop(0, AHEAD)
        def _(c):
            prepare_gate_up(c)

        for d in (1, 2, 3):
            token_arrival(0, d).wait_recv()
        def remote(src, dst, send, recv, other):
            return pltpu.make_async_remote_copy(
                src_ref=src, dst_ref=dst, send_sem=send, recv_sem=recv,
                device_id={"narrow": other}, device_id_type=MESH)

        def sib_copy(v):
            return remote(sibs.at[v], sibr.at[v], sib_s.at[v], sib_r.at[v], sib)

        def x_copy(v):
            return remote(xs.at[v], xr.at[v], x_s.at[v], x_r.at[v], peer)

        def hid_sib(v, which):
            return remote(hid.at[v, which], hid.at[v, which], hs_s.at[v], hs_r.at[v], sib)

        def hid_x(v, which):
            return remote(hid.at[v, which], hid.at[v, which], hx_s.at[v], hx_r.at[v], peer)

        def hid_forward(v, which):
            return remote(hid.at[v, which], hid.at[v, which], hf_s.at[v], hf_r.at[v], sib)

        def share_at(j):
            return pl.ds(pl.multiple_of(j * share, share), share)

        units = HALVES * chunks

        def stage_partial(v):
            slot = v % SLOTS
            h, c = v // chunks, v % chunks
            half_tokens = tokall[h]
            pbuf[slot, :, 0:CHUNK] = jnp.dot(half_tokens, gbuf[c], preferred_element_type=jnp.float32)
            pbuf[slot, :, CHUNK:] = jnp.dot(half_tokens, ubuf[c], preferred_element_type=jnp.float32)
            for side in range(2):
                sibs[v, side] = pbuf[slot, share_at(2 * side + 1 - k), :].astype(jnp.bfloat16)
            sib_copy(v).start()

        def stage_chip_sum(v):
            slot = v % SLOTS
            sib_copy(v).wait_recv()
            xs[v] = (pbuf[slot, share_at(peer), :] + sibr[v, 1 - x].astype(jnp.float32)).astype(jnp.bfloat16)
            x_copy(v).start()
            own[v] = pbuf[slot, share_at(n), :] + sibr[v, x].astype(jnp.float32)

        def stage_hidden(v):
            x_copy(v).wait_recv()
            both = own[v] + xr[v].astype(jnp.float32)
            g, u = both[:, :CHUNK], both[:, CHUNK:]
            hid[v, n] = (g / (1.0 + jnp.exp(-g)) * u).astype(jnp.bfloat16)
            hid_x(v, n).start()
            hid_sib(v, n).start()

        def stage_forward(v):
            hid_x(v, peer).wait_recv()
            hid_forward(v, peer).start()

        def z_copy(h, q, d):
            return pltpu.make_async_remote_copy(
                src_ref=zs.at[h, q, d - 1], dst_ref=zr.at[h, q, d - 1],
                send_sem=z_s.at[h, q, d - 1], recv_sem=z_r.at[h, q, d - 1],
                device_id={"wide": (w + d) % n_wide}, device_id_type=MESH)

        def stage_down(v):
            h, c = v // chunks, v % chunks

            hid_sib(v, sib).wait_recv()
            hid_forward(v, diag).wait_recv()

            @pl.loop(0, depth // PIECE)
            def _(q):
                cols = pl.ds(pl.multiple_of(q * PIECE, PIECE), PIECE)
                hidden = hid[v].reshape(n_wide * share, CHUNK)
                acc[h, :, cols] += jnp.dot(hidden, dbuf[c, :, cols], preferred_element_type=jnp.float32)

                @pl.when(c == chunks - 1)
                def _():
                    for d in (2, 3, 1):
                        zs[h, q, d - 1] = acc[h, share_at((w + d) % n_wide), cols].astype(jnp.bfloat16)
                        z_copy(h, q, d).start()

        def staged(t, lag, stage):
            @pl.when((t >= lag) & (t < chunks + lag))
            def _():
                stage(t - lag)

        @pl.loop(0, 2 * chunks + EXTRA)
        def _(t):
            @pl.when((t >= AHEAD) & (t < chunks))
            def _():
                prepare_gate_up(t)

            staged(t, 0, stage_partial)

            @pl.when((t >= chunks) & (t < 2 * chunks))
            def _():
                prepare_down(t - chunks)

            staged(t, SUM_LAG, stage_chip_sum)
            staged(t, HIDDEN_LAG, stage_hidden)
            staged(t, HIDDEN_LAG + FORWARD, stage_forward)
            staged(t, chunks + EXTRA, stage_down)

        for h in range(HALVES):
            rows_at = pl.ds(h * share, share)

            @pl.loop(0, depth // PIECE)
            def _(q):
                cols = pl.ds(pl.multiple_of(q * PIECE, PIECE), PIECE)
                total = acc[h, share_at(w), cols]
                for d in (1, 2, 3):
                    z_copy(h, q, d).wait_recv()
                    total = total + zr[h, q, d - 1].astype(jnp.float32)
                out[rows_at, cols] = total.astype(jnp.bfloat16)

        for h in range(HALVES):
            for d in (1, 2, 3):
                token_copy(h, d).wait_send()

        @pl.loop(0, units)
        def _(v):
            sib_copy(v).wait_send()
            x_copy(v).wait_send()
            hid_x(v, n).wait_send()
            hid_sib(v, n).wait_send()
            hid_forward(v, peer).wait_send()

        for h in range(HALVES):
            @pl.loop(0, depth // PIECE)
            def _(q):
                for d in (1, 2, 3):
                    z_copy(h, q, d).wait_send()

    return kernel


def fused_body(n_wide):
    def body(tokens, gate_weight, up_weight, down_weight, gate_keep, up_keep, down_keep):
        rows, depth = tokens.shape
        ff = gate_weight.shape[1]
        chunks = ff // CHUNK
        pieces = depth // PIECE
        share = rows // HALVES
        units = HALVES * chunks
        bf, f32 = jnp.bfloat16, jnp.float32
        vmem = pl.BlockSpec(memory_space=pltpu.VMEM)
        anywhere = pl.BlockSpec(memory_space=pl.ANY)
        dma = pltpu.SemaphoreType.DMA
        return pl.pallas_call(
            make_kernel(rows, n_wide, depth, ff, chunks),
            out_shape=jax.ShapeDtypeStruct((rows, depth), bf),
            in_specs=[vmem, anywhere, anywhere, anywhere, vmem, vmem, vmem],
            out_specs=vmem,
            scratch_shapes=[
                pltpu.VMEM((HALVES, n_wide * share, depth), bf),
                pltpu.VMEM((chunks, depth, CHUNK), bf),
                pltpu.VMEM((chunks, depth, CHUNK), bf),
                pltpu.VMEM((chunks, CHUNK, depth), bf),
                pltpu.VMEM((depth // BLOCK, ff), f32),
                pltpu.VMEM((depth // BLOCK, ff), f32),
                pltpu.VMEM((ff // BLOCK, depth), f32),
                pltpu.VMEM((SLOTS, n_wide * share, 2 * CHUNK), f32),
                pltpu.VMEM((units, 2, share, 2 * CHUNK), bf),
                pltpu.VMEM((units, 2, share, 2 * CHUNK), bf),
                pltpu.VMEM((units, share, 2 * CHUNK), f32),
                pltpu.VMEM((units, share, 2 * CHUNK), bf),
                pltpu.VMEM((units, share, 2 * CHUNK), bf),
                pltpu.VMEM((units, 4, share, CHUNK), bf),
                pltpu.VMEM((HALVES, n_wide * share, depth), f32),
                pltpu.VMEM((HALVES, pieces, n_wide - 1, share, PIECE), bf),
                pltpu.VMEM((HALVES, pieces, n_wide - 1, share, PIECE), bf),
                dma((HALVES, n_wide - 1)), dma((HALVES, n_wide - 1)),
                dma((chunks,)), dma((chunks,)), dma((chunks,)),
                dma((units,)), dma((units,)), dma((units,)), dma((units,)),
                dma((units,)), dma((units,)), dma((units,)), dma((units,)),
                dma((units,)), dma((units,)),
                dma((HALVES, pieces, n_wide - 1)), dma((HALVES, pieces, n_wide - 1)),
            ],
            compiler_params=pltpu.CompilerParams(
                collective_id=0, has_side_effects=True, vmem_limit_bytes=VMEM_LIMIT),
        )(tokens, gate_weight, up_weight, down_weight, gate_keep, up_keep, down_keep)

    return body


def solution(mesh):
    in_specs = (
        P(("groups", "wide"), "narrow"),
        P("narrow", "wide"),
        P("narrow", "wide"),
        P("wide", "narrow"),
        P("narrow", "wide"),
        P("narrow", "wide"),
        P("wide", "narrow"),
    )
    out_specs = P(("groups", "wide"), "narrow")
    fits = mesh.shape["wide"] == 4 and mesh.shape["narrow"] == 4
    body = fused_body(mesh.shape["wide"]) if fits else general_body
    return jax.shard_map(body, mesh=mesh, in_specs=in_specs, out_specs=out_specs, check_vma=False)
```
